32 devices in a mesh: replica: 4 (over y, core), fsdp: 4 (over z), tensor: 2 (over x).
Axes of the slice: x: 2, y: 2, z: 4, core: 2. Of those that a mesh axis runs over, the one named last changes fastest.
Arguments:
- cotangent: bfloat16 [4096, 4096], P(('replica', 'fsdp'), 'tensor'), may hold values from -6 to 6
- gate_pre: bfloat16 [4096, 14336], P(('replica', 'fsdp'), 'tensor'), may hold values from -6 to 6
- up_pre: bfloat16 [4096, 14336], P(('replica', 'fsdp'), 'tensor'), may hold values from -6 to 6
- down_weight: bfloat16 [14336, 4096], P('tensor', 'fsdp'), may hold values from -0.09375 to 0.09375
- projector: bfloat16 [4096, 512], P('tensor', 'fsdp'), may hold values from -0.09375 to 0.09375
Outputs:
- grad_gate: bfloat16 [4096, 14336], P(('replica', 'fsdp'), 'tensor')
- grad_up: bfloat16 [4096, 14336], P(('replica', 'fsdp'), 'tensor')
- projected_grad: float32 [512, 14336], P('fsdp', 'tensor')
The draws below stay inside these ranges and needn't reach their ends.
All inputs are finite; a program needn't handle non-finite values.
Results may differ from the reference program's by a relative error of at most 0.0049.
Values may be sent and summed in bfloat16 or wider, within the bound.
No kernel may reach another device: no remote copies, remote signals or barrier semaphores. Data moves between devices by JAX's collectives and lax.ppermute only.
A program may use at most 192 MiB of HBM per device.

```python
import math
import jax
import jax.numpy as jnp
from jax import lax

D = 4096
FF = 14336
RANK = 512
TOKENS = 4096


def level_of(rng, dims, shards, low, largest):
    factor_of, own = 1.0, jax.random.fold_in(rng, 6)
    for axis_at, parts in shards:
        steps = jnp.exp(jax.random.uniform(jax.random.fold_in(own, axis_at), (parts,), jnp.float32, low / len(shards), largest / len(shards)))
        factor_of = factor_of * jnp.repeat(steps, dims[axis_at] // parts).reshape([-1 if axis == axis_at else 1 for axis in range(len(dims))])
    return factor_of


def normal_values(own_key, shape, scale, reach, pieces=(), kind=jnp.bfloat16):
    drawn = scale * jax.random.normal(own_key, shape, jnp.float32)
    if pieces:
        drawn = drawn * level_of(own_key, shape, pieces, -0.22, 0.18)
    return jnp.clip(drawn, -reach, reach).astype(kind)


def setup_inputs(seed: int = 0) -> dict:
    arg_keys = jax.random.split(jax.random.key(seed), 6)
    return {
        "cotangent": normal_values(arg_keys[0], (TOKENS, D), 1.0, 6.0, ((0, 16), (1, 2))),
        "gate_pre": normal_values(arg_keys[1], (TOKENS, FF), 1.0, 6.0, ((0, 16), (1, 2))),
        "up_pre": normal_values(arg_keys[2], (TOKENS, FF), 1.0, 6.0, ((0, 16), (1, 2))),
        "down_weight": normal_values(arg_keys[3], (FF, D), D ** -0.5, 0.09375, ((0, 2), (1, 4))),
        "projector": normal_values(arg_keys[4], (D, RANK), D ** -0.5, 0.09375, ((0, 2), (1, 4))),
    }


def reference(cotangent, gate_pre, up_pre, down_weight, projector):
    block_rows = math.gcd(TOKENS, 1024)
    nblocks = TOKENS // block_rows
    cot_blocks = cotangent.reshape(nblocks, block_rows, D)
    gate_blocks = gate_pre.reshape(nblocks, block_rows, FF)
    up_blocks = up_pre.reshape(nblocks, block_rows, FF)
    down_trans = down_weight.T

    def one_block(running, inputs_block):
        cot_rows, gate_rows, up_rows = inputs_block
        hidden_grad = jnp.dot(cot_rows, down_trans, preferred_element_type=jnp.float32)
        gate_float = gate_rows.astype(jnp.float32)
        up_float = up_rows.astype(jnp.float32)
        sigma = jax.nn.sigmoid(gate_float)
        activated = gate_float * sigma
        hidden = (activated * up_float).astype(jnp.bfloat16)
        grad_up = (hidden_grad * activated).astype(jnp.bfloat16)
        grad_gate = (hidden_grad * up_float * sigma * (1.0 + gate_float * (1.0 - sigma))).astype(jnp.bfloat16)
        low_rank = jnp.dot(cot_rows, projector, preferred_element_type=jnp.float32).astype(jnp.bfloat16)
        term_block = jnp.dot(low_rank.T, hidden, preferred_element_type=jnp.float32)
        return (running + term_block, (grad_gate, grad_up))
    start = jnp.zeros((RANK, FF), jnp.float32)
    total, outputs = lax.scan(one_block, start, (cot_blocks, gate_blocks, up_blocks))
    grad_gate = outputs[0].reshape(TOKENS, FF)
    grad_up = outputs[1].reshape(TOKENS, FF)
    projected_grad = total * (1.0 / math.sqrt(TOKENS))
    return (grad_gate, grad_up, projected_grad)
```

```python
import functools
import math

import jax
import jax.numpy as jnp
from jax import lax
from jax.experimental import pallas as pl
from jax.experimental.pallas import tpu as pltpu
from jax.sharding import PartitionSpec as P

AXES = ("replica", "fsdp", "tensor")
VMEM_BYTES = 40 * 1024 * 1024


def general(cotangent, gate_pre, up_pre, down_weight, projector):
    whole = lax.all_gather(cotangent, "tensor", axis=1, tiled=True)
    local_rows = cotangent.shape[0]
    hidden_cols = gate_pre.shape[1]
    hidden_grad = lax.dot_general(
        whole,
        lax.all_gather(down_weight, "fsdp", axis=1, tiled=True),
        (((1,), (1,)), ((), ())),
        preferred_element_type=jnp.float32,
    )
    projector_full_cols = lax.all_gather(projector, "fsdp", axis=1, tiled=True)
    partial_rank = jnp.dot(cotangent, projector_full_cols, preferred_element_type=jnp.float32)
    low_rank = lax.psum(partial_rank, "tensor").astype(jnp.bfloat16)
    gate_float = gate_pre.astype(jnp.float32)
    up_float = up_pre.astype(jnp.float32)
    sigma = jax.nn.sigmoid(gate_float)
    activated = gate_float * sigma
    hidden = (activated * up_float).astype(jnp.bfloat16)
    grad_up = (hidden_grad * activated).astype(jnp.bfloat16)
    grad_gate = (hidden_grad * up_float * sigma * (1.0 + gate_float * (1.0 - sigma))).astype(
        jnp.bfloat16
    )
    replicas = lax.axis_size("replica")
    shards = lax.axis_size("fsdp")
    token_total = local_rows * replicas * shards
    scale_factor = 1.0 / math.sqrt(token_total)
    partial_grad = (
        lax.dot_general(
            low_rank, hidden, (((0,), (0,)), ((), ())), preferred_element_type=jnp.float32
        )
        * scale_factor
    )
    rank_size = partial_grad.shape[0]
    piece_rows = rank_size // (shards * replicas)
    reordered = partial_grad.reshape(shards, replicas, piece_rows, hidden_cols)
    reordered = jnp.swapaxes(reordered, 0, 1).reshape(rank_size, hidden_cols)
    joint_piece = lax.psum_scatter(reordered, ("replica", "fsdp"), scatter_dimension=0, tiled=True)
    projected_grad = lax.all_gather(joint_piece, "replica", axis=0, tiled=True)
    return (grad_gate, grad_up, projected_grad)


def chunk_plan(quarter, unit, count):
    units = quarter // unit
    each = -(-units // count)
    plan, at = [], 0
    while at < units:
        width = min(each, units - at)
        plan.append((at * unit, width * unit))
        at += width
    return plan


def mix_kernel(order, near, far, w0, w1, w2, w3, out):
    width = w0.shape[1]
    for side, tokens in enumerate((near, far)):
        total = None
        for b, w in enumerate((w0, w1, w2, w3)):
            at = pl.multiple_of(order[b] * width, width)
            term = lax.dot_general(
                tokens[:, pl.ds(at, width)],
                w[...],
                (((1,), (1,)), ((), ())),
                preferred_element_type=jnp.float32,
            )
            total = term if total is None else total + term
        out[side, 0] = total.astype(out.dtype)


def mix(order, near, far, blocks, leaf, rows):
    units = blocks[0].shape[0]
    lines = near.shape[0] // (2 * rows)
    features = near.shape[1]
    token_spec = pl.BlockSpec((rows, features), lambda i, order: (2 * i + leaf, 0))
    weight_spec = pl.BlockSpec(blocks[0].shape, lambda i, order: (0, 0))
    return pl.pallas_call(
        mix_kernel,
        out_shape=jax.ShapeDtypeStruct((2, lines, rows, units), jnp.bfloat16),
        grid_spec=pltpu.PrefetchScalarGridSpec(
            num_scalar_prefetch=1,
            grid=(lines,),
            in_specs=[token_spec, token_spec] + [weight_spec] * len(blocks),
            out_specs=pl.BlockSpec((2, 1, rows, units), lambda i, order: (0, i, 0, 0)),
        ),
        compiler_params=pltpu.CompilerParams(vmem_limit_bytes=VMEM_BYTES),
        cost_estimate=pl.CostEstimate(
            flops=2 * near.shape[0] * features * units,
            bytes_accessed=2 * (near.size + units * features + near.shape[0] * units),
            transcendentals=0,
        ),
        name="hidden_grad_chunk",
    )(order, near, far, *blocks)


def grads_kernel(position, p0, p1, p2, p3, gate, up, *refs):
    grad_gate, grad_up = refs[-2:]
    for d, piece in enumerate((p0, p1, p2, p3)):

        @pl.when(pl.program_id(0) == d)
        def _():
            gate_float = gate[...].astype(jnp.float32)
            up_float = up[...].astype(jnp.float32)
            hidden_grad = piece[...].astype(jnp.float32)
            sigma = jax.nn.sigmoid(gate_float)
            grad_up[...] = (hidden_grad * (gate_float * sigma)).astype(grad_up.dtype)
            grad_gate[...] = (
                hidden_grad * up_float * sigma * (1.0 + gate_float * (1.0 - sigma))
            ).astype(grad_gate.dtype)


def grads(position, pieces, gate, up, kept, offset, quarter, unit):
    rows, width = pieces[0].shape
    subs = width // unit

    def piece_map(d):
        return lambda i, j, position: (0, jnp.where(i == d, j, jnp.where(i < d, 0, subs - 1)))

    def column_map(i, j, position):
        return (0, (position[0] ^ i) * (quarter // unit) + offset // unit + j)

    columns = pl.BlockSpec((rows, unit), column_map)
    anywhere = pl.BlockSpec(memory_space=pl.ANY)
    return pl.pallas_call(
        grads_kernel,
        out_shape=[jax.ShapeDtypeStruct(gate.shape, jnp.bfloat16)] * 2,
        grid_spec=pltpu.PrefetchScalarGridSpec(
            num_scalar_prefetch=1,
            grid=(4, subs),
            in_specs=[pl.BlockSpec((rows, unit), piece_map(d)) for d in range(4)]
            + [columns, columns]
            + [anywhere] * len(kept),
            out_specs=[columns, columns],
        ),
        input_output_aliases={7: 0, 8: 1} if kept else {},
        compiler_params=pltpu.CompilerParams(vmem_limit_bytes=VMEM_BYTES),
        cost_estimate=pl.CostEstimate(
            flops=4 * 12 * rows * width,
            bytes_accessed=4 * 10 * rows * width,
            transcendentals=4 * rows * width,
        ),
        name="grads_chunk",
    )(position, *pieces, gate, up, *kept)


def ranks_kernel(position, low, gate, up, out):
    gate_float = gate[...].astype(jnp.float32)
    activated = gate_float * jax.nn.sigmoid(gate_float)
    hidden = (activated * up[...].astype(jnp.float32)).astype(jnp.bfloat16)
    out[0] = lax.dot_general(
        low[...], hidden, (((0,), (0,)), ((), ())), preferred_element_type=jnp.float32
    ).astype(out.dtype)


def ranks(position, low, gate, up, swaps, quarter, kind):
    rows, rank = low.shape
    parts = 2 if quarter % 256 == 0 else 1
    width = quarter // parts
    first, step = swaps[0], swaps[0] ^ swaps[1]

    def column_map(i, j, position):
        return (0, (position[0] ^ first ^ (i * step)) * parts + j)

    columns = pl.BlockSpec((rows, width), column_map)
    return pl.pallas_call(
        ranks_kernel,
        out_shape=jax.ShapeDtypeStruct((2, rank, quarter), kind),
        grid_spec=pltpu.PrefetchScalarGridSpec(
            num_scalar_prefetch=1,
            grid=(2, parts),
            in_specs=[pl.BlockSpec(low.shape, lambda i, j, position: (0, 0)), columns, columns],
            out_specs=pl.BlockSpec((1, rank, width), lambda i, j, position: (i, 0, j)),
        ),
        compiler_params=pltpu.CompilerParams(vmem_limit_bytes=VMEM_BYTES),
        cost_estimate=pl.CostEstimate(
            flops=2 * rows * rank * 2 * quarter,
            bytes_accessed=2 * quarter * (4 * rows + 4 * rank),
            transcendentals=2 * rows * quarter,
        ),
        name="rank_terms",
    )(position, low, gate, up)


def line(cotangent, gate_pre, up_pre, down_weight, projector):
    replicas, shards, tensors = (lax.axis_size(a) for a in AXES)
    r, f, t = (lax.axis_index(a) for a in AXES)
    rows = cotangent.shape[0]
    quarter = down_weight.shape[0] // replicas
    last = shards - 1
    inner = (f != 0) & (f != last)
    bf16, f32 = jnp.bfloat16, jnp.float32

    def send(x, rule):
        pairs = []
        for a in range(replicas):
            for b in range(shards):
                for c in range(tensors):
                    to = rule(a, b, c)
                    if to is not None:
                        here = (a * shards + b) * tensors + c
                        pairs.append((here, (to[0] * shards + to[1]) * tensors + to[2]))
        return lax.ppermute(x, AXES, pairs)

    def is_inner(b):
        return 0 < b < last

    to_inner = lambda a, b, c: None if is_inner(b) else (a, b ^ 1, c)
    to_outer = lambda a, b, c: (a, b ^ 1, c) if is_inner(b) else None
    across = lambda a, b, c: (a, last - b, c) if is_inner(b) else None
    inner_y = lambda a, b, c: (a ^ 2, b, c) if is_inner(b) else None
    inner_core = lambda a, b, c: (a ^ 1, b, c) if is_inner(b) else None
    inner_x = lambda a, b, c: (a, b, c ^ 1) if is_inner(b) else None
    swap = lambda d: lambda a, b, c: (a ^ d, b, c)
    swap_x = lambda a, b, c: (a, b, c ^ 1)

    position = jnp.reshape(r, (1,)).astype(jnp.int32)

    unit = 256 if quarter % 256 == 0 else 128
    plan = chunk_plan(quarter, unit, 4)
    blocks = []
    for offset, width in plan:
        own = lax.dynamic_slice_in_dim(down_weight, r * quarter + offset, width, 0)
        edge = send(own, to_inner)
        blocks.append((own, edge, send(own, across), send(edge, across)))

    outer_rows = send(cotangent, to_inner)
    mine = (cotangent, outer_rows, send(cotangent, inner_y), send(outer_rows, inner_y))
    near = jnp.concatenate(
        [jnp.concatenate([m, send(m, inner_x)], axis=1) for m in mine], axis=0
    )
    far = send(near, inner_core)

    projector_rows = projector.shape[0] // replicas
    part = lax.dynamic_slice_in_dim(projector, r * projector_rows, projector_rows, 0)
    part = lax.all_gather(part, "fsdp", axis=1, tiled=True)
    projector_full = lax.all_gather(part, "replica", axis=0, tiled=True)
    partial_rank = jnp.dot(cotangent, projector_full, preferred_element_type=f32)
    low = (partial_rank + send(partial_rank, swap_x)).astype(bf16)

    rank_size = low.shape[1]
    away = ranks(position, low, gate_pre, up_pre, (1, 3), quarter, bf16)
    keep = ranks(position, low, gate_pre, up_pre, (0, 2), quarter, f32)
    keep = keep + send(away, swap(1)).astype(f32)
    mine = keep[0] + send(keep[1].astype(bf16), swap(2)).astype(f32)
    piece = rank_size // shards
    half = rank_size // 2
    outgoing = jnp.where(f == 0, mine[piece:], mine[:-piece]).astype(bf16)
    got = send(outgoing, to_inner).astype(f32)
    pad = jnp.zeros((piece, quarter), f32)
    joined = mine + jnp.where(
        f < shards // 2, jnp.concatenate([pad, got]), jnp.concatenate([got, pad])
    )
    low_half, high_half = joined[:half], joined[half:]
    lower = f < shards // 2
    crossed = send(jnp.where(lower, high_half, low_half).astype(bf16), across).astype(f32)
    pair = jnp.where(lower, low_half, high_half) + crossed
    for_inner = jnp.where(lower, pair[piece:], pair[:piece])
    for_outer = jnp.where(lower, pair[:piece], pair[piece:]).astype(bf16)
    returned = send(for_outer, to_outer).astype(f32)
    own_piece = jnp.where(lower, mine[:piece], mine[-piece:])
    scale_factor = 1.0 / math.sqrt(rows * replicas * shards)
    final = (jnp.where(inner, for_inner, own_piece + returned) * scale_factor).astype(bf16)
    two = jnp.stack([final, send(final, swap(2))])
    other = send(two, swap(1))
    projected_grad = jnp.zeros((piece, gate_pre.shape[1]), f32)
    for d, q in ((0, two[0]), (2, two[1]), (1, other[0]), (3, other[1])):
        projected_grad = lax.dynamic_update_slice(
            projected_grad, q.astype(f32), (0, (r ^ d) * quarter)
        )

    halves = shards // tensors
    order = jnp.stack(
        [((b // halves) ^ t) * halves + b % halves for b in (f, f ^ 1, last - f, (last - f) ^ 1)]
    ).astype(jnp.int32)
    kept = ()
    for (offset, width), chunk in zip(plan, blocks):
        outer_part = mix(order, near, far, chunk, 1, rows)
        inner_part = mix(order, near, far, chunk, 0, rows)
        home = jnp.where(inner, inner_part, send(outer_part, to_outer))
        pieces = [
            home[0, 0],
            send(home[1, 0], swap(1)),
            send(home[0, 1], swap(2)),
            send(home[1, 1], swap(3)),
        ]
        kept = grads(position, pieces, gate_pre, up_pre, kept, offset, quarter, unit)
    return (kept[0], kept[1], projected_grad)


def solution(mesh):
    sizes = tuple(mesh.shape[a] for a in AXES)
    placed = (
        P(("replica", "fsdp"), "tensor"),
        P(("replica", "fsdp"), "tensor"),
        P(("replica", "fsdp"), "tensor"),
        P("tensor", "fsdp"),
        P("tensor", "fsdp"),
    )
    return jax.shard_map(
        line if sizes == (4, 4, 2) else general,
        mesh=mesh,
        in_specs=placed,
        out_specs=(
            P(("replica", "fsdp"), "tensor"),
            P(("replica", "fsdp"), "tensor"),
            P("fsdp", "tensor"),
        ),
        check_vma=False,
    )
```

```python
import functools
import math

import jax
import jax.numpy as jnp
from jax import lax
from jax.experimental import pallas as pl
from jax.experimental.pallas import tpu as pltpu
from jax.sharding import PartitionSpec as P

AXES = ("replica", "fsdp", "tensor")
VMEM_BYTES = 40 * 1024 * 1024
LIGHT = pl.CostEstimate(flops=0, bytes_accessed=0, transcendentals=0)


def general(cotangent, gate_pre, up_pre, down_weight, projector):
    whole = lax.all_gather(cotangent, "tensor", axis=1, tiled=True)
    local_rows = cotangent.shape[0]
    hidden_cols = gate_pre.shape[1]
    hidden_grad = lax.dot_general(
        whole,
        lax.all_gather(down_weight, "fsdp", axis=1, tiled=True),
        (((1,), (1,)), ((), ())),
        preferred_element_type=jnp.float32,
    )
    projector_full_cols = lax.all_gather(projector, "fsdp", axis=1, tiled=True)
    partial_rank = jnp.dot(cotangent, projector_full_cols, preferred_element_type=jnp.float32)
    low_rank = lax.psum(partial_rank, "tensor").astype(jnp.bfloat16)
    gate_float = gate_pre.astype(jnp.float32)
    up_float = up_pre.astype(jnp.float32)
    sigma = jax.nn.sigmoid(gate_float)
    activated = gate_float * sigma
    hidden = (activated * up_float).astype(jnp.bfloat16)
    grad_up = (hidden_grad * activated).astype(jnp.bfloat16)
    grad_gate = (hidden_grad * up_float * sigma * (1.0 + gate_float * (1.0 - sigma))).astype(
        jnp.bfloat16
    )
    replicas = lax.axis_size("replica")
    shards = lax.axis_size("fsdp")
    token_total = local_rows * replicas * shards
    scale_factor = 1.0 / math.sqrt(token_total)
    partial_grad = (
        lax.dot_general(
            low_rank, hidden, (((0,), (0,)), ((), ())), preferred_element_type=jnp.float32
        )
        * scale_factor
    )
    rank_size = partial_grad.shape[0]
    piece_rows = rank_size // (shards * replicas)
    reordered = partial_grad.reshape(shards, replicas, piece_rows, hidden_cols)
    reordered = jnp.swapaxes(reordered, 0, 1).reshape(rank_size, hidden_cols)
    joint_piece = lax.psum_scatter(reordered, ("replica", "fsdp"), scatter_dimension=0, tiled=True)
    projected_grad = lax.all_gather(joint_piece, "replica", axis=0, tiled=True)
    return (grad_gate, grad_up, projected_grad)


def chunk_plan(quarter, unit, count):
    units = quarter // unit
    each = -(-units // count)
    plan, at = [], 0
    while at < units:
        width = min(each, units - at)
        plan.append((at * unit, width * unit))
        at += width
    return plan


def cover(start, count, step):
    blocks = []
    while count:
        size = max(n for n in range(step, count + 1, step) if start % n == 0)
        blocks.append((size, start // size))
        start, count = start + size, count - size
    return blocks


def mix_kernel(held, position, tokens, *refs):
    kept, sent = refs[-2:]
    rows = kept.shape[1]
    at = position[1]
    total = None
    for where, pieces in ((at, refs[:held]), (1 - at, refs[held:-2])):
        w = jnp.concatenate([piece[...] for piece in pieces], axis=0)
        term = lax.dot_general(
            tokens[0, where], w, (((1,), (1,)), ((), ())), preferred_element_type=jnp.float32
        )
        total = term if total is None else total + term
    kept[0] = total[:rows]
    sent[0] = total[rows:].astype(sent.dtype)


def mix(position, tokens, weight, quarter, run, unit, pieces):
    replicas, _, both, _ = tokens.shape
    rows, block = both // 2, weight.shape[1]
    offset, units = run
    held = units // unit
    out_spec = pl.BlockSpec((1, rows, units), lambda i, position: (i, 0, 0))
    return pl.pallas_call(
        functools.partial(mix_kernel, held),
        out_shape=[
            jax.ShapeDtypeStruct((replicas, rows, units), jnp.float32),
            jax.ShapeDtypeStruct((replicas, rows, units), jnp.bfloat16),
        ],
        grid_spec=pltpu.PrefetchScalarGridSpec(
            num_scalar_prefetch=1,
            grid=(replicas,),
            in_specs=[
                pl.BlockSpec((1,) + tokens.shape[1:], lambda i, position: (position[0] ^ i, 0, 0, 0))
            ]
            + [
                pl.BlockSpec(
                    (unit, block),
                    lambda i, position, j=j: (position[0] * (quarter // unit) + offset // unit + j, 0),
                )
                for j in range(held)
            ]
            + [
                pl.BlockSpec((size, block), lambda i, position, index=index: (index, 0))
                for _, size, index in pieces
            ],
            out_specs=[out_spec, out_spec],
        ),
        compiler_params=pltpu.CompilerParams(vmem_limit_bytes=60 * 1024 * 1024),
        cost_estimate=LIGHT,
        name="hidden_grad_chunk",
    )(position, tokens, *[weight] * held, *(w for w, _, _ in pieces))


def grads_kernel(position, p0, p1, p2, p3, gate, up, *refs):
    grad_gate, grad_up = refs[-2:]
    for d, piece in enumerate((p0, p1, p2, p3)):

        @pl.when(pl.program_id(0) == d)
        def _():
            gate_float = gate[...].astype(jnp.float32)
            up_float = up[...].astype(jnp.float32)
            hidden_grad = piece[...].astype(jnp.float32)
            sigma = jax.nn.sigmoid(gate_float)
            grad_up[...] = (hidden_grad * (gate_float * sigma)).astype(grad_up.dtype)
            grad_gate[...] = (
                hidden_grad * up_float * sigma * (1.0 + gate_float * (1.0 - sigma))
            ).astype(grad_gate.dtype)


def grads(position, pieces, gate, up, kept, offset, quarter, unit):
    rows, width = pieces[0].shape
    subs = width // unit

    def piece_map(d):
        return lambda i, j, position: (0, jnp.where(i == d, j, jnp.where(i < d, 0, subs - 1)))

    def column_map(i, j, position):
        return (0, (position[0] ^ i) * (quarter // unit) + offset // unit + j)

    columns = pl.BlockSpec((rows, unit), column_map)
    anywhere = pl.BlockSpec(memory_space=pl.ANY)
    return pl.pallas_call(
        grads_kernel,
        out_shape=[jax.ShapeDtypeStruct(gate.shape, jnp.bfloat16)] * 2,
        grid_spec=pltpu.PrefetchScalarGridSpec(
            num_scalar_prefetch=1,
            grid=(4, subs),
            in_specs=[pl.BlockSpec((rows, unit), piece_map(d)) for d in range(4)]
            + [columns, columns]
            + [anywhere] * len(kept),
            out_specs=[columns, columns],
        ),
        input_output_aliases={7: 0, 8: 1} if kept else {},
        compiler_params=pltpu.CompilerParams(vmem_limit_bytes=VMEM_BYTES),
        cost_estimate=LIGHT,
        name="grads_chunk",
    )(position, *pieces, gate, up, *kept)


def hidden_kernel(position, gate, up, *outs):
    gate_float = gate[...].astype(jnp.float32)
    activated = gate_float * jax.nn.sigmoid(gate_float)
    hidden = (activated * up[...].astype(jnp.float32)).astype(jnp.bfloat16)
    for d, out in enumerate(outs):

        @pl.when(pl.program_id(0) == d)
        def _():
            out[...] = hidden


def hidden_quarters(position, gate, up, quarter):
    rows = gate.shape[0]
    columns = pl.BlockSpec((rows, quarter), lambda i, position: (0, position[0] ^ i))
    return pl.pallas_call(
        hidden_kernel,
        out_shape=[jax.ShapeDtypeStruct((rows, quarter), jnp.bfloat16)] * 4,
        grid_spec=pltpu.PrefetchScalarGridSpec(
            num_scalar_prefetch=1,
            grid=(4,),
            in_specs=[columns, columns],
            out_specs=[pl.BlockSpec((rows, quarter), lambda i, position: (0, 0))] * 4,
        ),
        compiler_params=pltpu.CompilerParams(vmem_limit_bytes=VMEM_BYTES),
        cost_estimate=LIGHT,
        name="hidden_quarters",
    )(position, gate, up)


def terms_kernel(*refs):
    total = None
    count = len(refs) // 2
    for low, hidden in zip(refs[:count], refs[count:-1]):
        term = lax.dot_general(
            low[...], hidden[...], (((0,), (0,)), ((), ())), preferred_element_type=jnp.float32
        )
        total = term if total is None else total + term
    refs[-1][...] = total


def rank_terms(low, hidden):
    rows, quarter = hidden[0].shape
    rank = low[0].shape[1]
    parts = 2 if quarter % 256 == 0 else 1
    width = quarter // parts
    return pl.pallas_call(
        terms_kernel,
        out_shape=jax.ShapeDtypeStruct((rank, quarter), jnp.float32),
        grid=(parts,),
        in_specs=[pl.BlockSpec((rows, rank), lambda i: (0, 0))] * len(low)
        + [pl.BlockSpec((rows, width), lambda i: (0, i))] * len(hidden),
        out_specs=pl.BlockSpec((rank, width), lambda i: (0, i)),
        compiler_params=pltpu.CompilerParams(vmem_limit_bytes=VMEM_BYTES),
        cost_estimate=LIGHT,
        name="rank_terms",
    )(*low, *hidden)


def line(cotangent, gate_pre, up_pre, down_weight, projector):
    replicas, shards, tensors = (lax.axis_size(a) for a in AXES)
    r, f, t = (lax.axis_index(a) for a in AXES)
    rows = cotangent.shape[0]
    quarter = down_weight.shape[0] // replicas
    block = down_weight.shape[1]
    bf16, f32 = jnp.bfloat16, jnp.float32

    def send(x, move):
        pairs = []
        for a in range(replicas):
            for b in range(shards):
                for c in range(tensors):
                    here = (a * shards + b) * tensors + c
                    there = ((a ^ move[0]) * shards + (b ^ move[1])) * tensors + (c ^ move[2])
                    pairs.append((here, there))
        return lax.ppermute(x, AXES, pairs)

    def after(x, *earlier):
        return lax.optimization_barrier((x, *earlier))[0]

    along, beyond, over_tensor = (0, 1, 0), (0, 2, 0), (0, 0, 1)
    odd, high = f % 2, f // 2
    position = jnp.stack([r, high]).astype(jnp.int32)
    unit = 256 if quarter % 256 == 0 else 128
    plan = chunk_plan(quarter, unit, 4)

    def spread(kept, part):
        total = (kept + part.astype(f32)).astype(bf16)
        return [total[0]] + [send(total[d], (d, 0, 0)) for d in range(1, 4)]

    def finish(k, pieces, written):
        return grads(position, pieces, gate_pre, up_pre, written, plan[k][0], quarter, unit)

    first = 128
    lengths = [first, plan[0][1] - first] + [count for _, count in plan[1:]]
    starts = [sum(lengths[:i]) for i in range(5)]
    own_rows = [
        lax.dynamic_slice_in_dim(down_weight, r * quarter + offset, count, 0)
        for offset, count in zip(starts, lengths)
    ]
    cross = [send(own_rows[0], beyond)]

    def chunk(k, *earlier):
        at, end = plan[k][0], plan[k][0] + plan[k][1]
        pieces = []
        for x, start, length in zip(cross, starts, lengths):
            low, high = max(at, start), min(end, start + length)
            if low < high:
                pieces += [(x, *found) for found in cover(low - start, high - low, first)]
        return mix(position, after(tokens, *earlier), down_weight, quarter, plan[k], unit, pieces)

    mine = lax.dynamic_slice_in_dim(cotangent, odd * block, block, 1)
    give = lax.dynamic_slice_in_dim(cotangent, (1 - odd) * block, block, 1)
    given = send(give, along)
    tokens = jnp.concatenate([mine, after(given, cross[0])], axis=0)
    tokens = lax.all_gather(tokens, ("replica", "tensor"))
    tokens = tokens.reshape((replicas, tensors) + tokens.shape[1:])
    tick = (cross[0], given)

    hidden = hidden_quarters(position, gate_pre, up_pre, quarter)
    met = {2: send(hidden[2], (2, 0, 0))}
    cross.append(send(after(own_rows[1], *tick), beyond))
    projector_rows = projector.shape[0] // replicas
    part = lax.dynamic_slice_in_dim(projector, r * projector_rows, projector_rows, 0)
    part = after(part, *tick)
    around = [part] + [send(part, (0, d, 0)) for d in (1, 2, 3)]
    cols = part.shape[1]
    part = jnp.zeros((projector_rows, shards * cols), bf16)
    for d, x in enumerate(around):
        part = lax.dynamic_update_slice(part, x, (0, (f ^ d) * cols))
    around = [part] + [send(part, (d, 0, 0)) for d in (1, 2, 3)]
    early = tick
    tick = (*around[1:], cross[1], met[2])

    cross.append(send(after(own_rows[2], *early), beyond))
    projector_full = jnp.zeros((projector.shape[0], part.shape[1]), bf16)
    for d, x in enumerate(after(around, *tick)):
        projector_full = lax.dynamic_update_slice(
            projector_full, x, ((r ^ d) * projector_rows, 0)
        )
    partial_rank = jnp.dot(cotangent, projector_full, preferred_element_type=f32)
    over_x = send(partial_rank, over_tensor)
    early = tick
    tick = (over_x,)

    low = (partial_rank + after(over_x, *tick)).astype(bf16)
    lows = [low] + [send(low, (d, 0, 0)) for d in (1, 2, 3)]
    kept, sent = [None] * 4, [None] * 4
    kept[0], sent[0] = chunk(0, *tick)
    parts = [send(sent[0], along)]
    tick = (sent[0], cross[2])

    cross.append(send(after(own_rows[3], *early), beyond))
    for d in (1, 3):
        met[d] = send(after(hidden[d], sent[0]), (d, 0, 0))
    kept[1], sent[1] = chunk(1, *tick)
    parts.append(send(sent[1], along))
    early = tick
    tick = (sent[1], cross[3])

    cross.append(send(after(own_rows[4], *early), beyond))
    total = rank_terms(after(lows, sent[1]), [hidden[0], met[1], met[2], met[3]])
    piece = low.shape[1] // shards
    total = total.reshape(2, 2, piece, quarter)
    theirs = jnp.where(odd == 0, total[:, 1], total[:, 0]).astype(bf16)
    total = jnp.where(odd == 0, total[:, 0], total[:, 1])
    stage = send(theirs, along)
    kept[2], sent[2] = chunk(2, *tick)
    parts.append(send(sent[2], along))
    pieces = [spread(after(kept[0], sent[2]), parts[0])]
    tick = (sent[2], theirs, *pieces[0][1:], cross[4])

    kept[3], sent[3] = chunk(3, *tick)
    parts.append(send(sent[3], along))
    total = total + after(stage, sent[3]).astype(f32)
    theirs = jnp.where(high == 0, total[1], total[0]).astype(bf16)
    total = jnp.where(high == 0, total[0], total[1])
    crossed = send(theirs, beyond)
    pieces.append(spread(after(kept[1], theirs), parts[1]))
    written = finish(0, after(pieces[0], theirs), ())
    tick = (written[0], *pieces[1][1:])

    pieces.append(spread(after(kept[2], *tick), parts[2]))
    written = finish(1, after(pieces[1], *tick), written)
    scale_factor = 1.0 / math.sqrt(rows * replicas * shards)
    final = ((total + after(crossed, *tick).astype(f32)) * scale_factor).astype(bf16)
    over_y = send(final, (2, 0, 0))
    tick = (parts[3], final, written[0])

    pieces.append(spread(after(kept[3], *tick), parts[3]))
    two = jnp.stack([final, over_y])
    other = send(after(two, *pieces[2][1:]), (1, 0, 0))
    written = finish(2, after(pieces[2], *tick), written)
    kept = finish(3, after(pieces[3], written[0]), written)
    projected_grad = jnp.zeros((piece, gate_pre.shape[1]), f32)
    for d, q in ((0, two[0]), (2, two[1]), (1, other[0]), (3, other[1])):
        projected_grad = lax.dynamic_update_slice(
            projected_grad, q.astype(f32), (0, (r ^ d) * quarter)
        )
    return (kept[0], kept[1], projected_grad)


def solution(mesh):
    sizes = tuple(mesh.shape[a] for a in AXES)
    placed = (
        P(("replica", "fsdp"), "tensor"),
        P(("replica", "fsdp"), "tensor"),
        P(("replica", "fsdp"), "tensor"),
        P("tensor", "fsdp"),
        P("tensor", "fsdp"),
    )
    return jax.shard_map(
        line if sizes == (4, 4, 2) else general,
        mesh=mesh,
        in_specs=placed,
        out_specs=(
            P(("replica", "fsdp"), "tensor"),
            P(("replica", "fsdp"), "tensor"),
            P("fsdp", "tensor"),
        ),
        check_vma=False,
    )
```

```python
import functools
import math

import jax
import jax.numpy as jnp
from jax import lax
from jax.experimental import pallas as pl
from jax.experimental.pallas import tpu as pltpu
from jax.sharding import PartitionSpec as P

AXES = ("replica", "fsdp", "tensor")
VMEM_BYTES = 40 * 1024 * 1024
LIGHT = pl.CostEstimate(flops=0, bytes_accessed=0, transcendentals=0)


def general(cotangent, gate_pre, up_pre, down_weight, projector):
    whole = lax.all_gather(cotangent, "tensor", axis=1, tiled=True)
    local_rows = cotangent.shape[0]
    hidden_cols = gate_pre.shape[1]
    hidden_grad = lax.dot_general(
        whole,
        lax.all_gather(down_weight, "fsdp", axis=1, tiled=True),
        (((1,), (1,)), ((), ())),
        preferred_element_type=jnp.float32,
    )
    projector_full_cols = lax.all_gather(projector, "fsdp", axis=1, tiled=True)
    partial_rank = jnp.dot(cotangent, projector_full_cols, preferred_element_type=jnp.float32)
    low_rank = lax.psum(partial_rank, "tensor").astype(jnp.bfloat16)
    gate_float = gate_pre.astype(jnp.float32)
    up_float = up_pre.astype(jnp.float32)
    sigma = jax.nn.sigmoid(gate_float)
    activated = gate_float * sigma
    hidden = (activated * up_float).astype(jnp.bfloat16)
    grad_up = (hidden_grad * activated).astype(jnp.bfloat16)
    grad_gate = (hidden_grad * up_float * sigma * (1.0 + gate_float * (1.0 - sigma))).astype(
        jnp.bfloat16
    )
    replicas = lax.axis_size("replica")
    shards = lax.axis_size("fsdp")
    token_total = local_rows * replicas * shards
    scale_factor = 1.0 / math.sqrt(token_total)
    partial_grad = (
        lax.dot_general(
            low_rank, hidden, (((0,), (0,)), ((), ())), preferred_element_type=jnp.float32
        )
        * scale_factor
    )
    rank_size = partial_grad.shape[0]
    piece_rows = rank_size // (shards * replicas)
    reordered = partial_grad.reshape(shards, replicas, piece_rows, hidden_cols)
    reordered = jnp.swapaxes(reordered, 0, 1).reshape(rank_size, hidden_cols)
    joint_piece = lax.psum_scatter(reordered, ("replica", "fsdp"), scatter_dimension=0, tiled=True)
    projected_grad = lax.all_gather(joint_piece, "replica", axis=0, tiled=True)
    return (grad_gate, grad_up, projected_grad)


def chunk_plan(quarter, unit, count):
    units = quarter // unit
    each = -(-units // count)
    plan, at = [], 0
    while at < units:
        width = min(each, units - at)
        plan.append((at * unit, width * unit))
        at += width
    return plan


def mix_kernel(position, tokens, own, cross, *refs):
    columns, out = refs[:-1], refs[-1]
    replicas, _, rows, block = tokens.shape
    at = position[1]
    unit = own.shape[0]
    step = pl.program_id(0)
    where = pl.ds(pl.multiple_of(step * unit, unit), unit)
    total = None
    for side, w in ((at, own[...]), (1 - at, cross[...])):
        x = tokens[:, side].reshape(replicas * rows, block)
        term = lax.dot_general(
            x, w, (((1,), (1,)), ((), ())), preferred_element_type=jnp.float32
        )
        total = term if total is None else total + term
    for a in range(replicas):
        out[position[0] ^ a, :, where] = total[a * rows : (a + 1) * rows].astype(out.dtype)
    if columns:
        width = columns[0].shape[1]

        @pl.when(step == 0)
        def _():
            total = None
            for side, p in enumerate(columns):
                x = tokens[:, side].reshape(replicas * rows, block)
                term = jnp.dot(x, p[...], preferred_element_type=jnp.float32)
                total = term if total is None else total + term
            for a in range(replicas):
                out[position[0] ^ a, :, out.shape[2] - width :] = total[
                    a * rows : (a + 1) * rows
                ].astype(out.dtype)


def mix(position, tokens, weight, quarter, run, unit, cross, columns, kind, cost):
    replicas, _, rows, _ = tokens.shape
    block = weight.shape[1]
    offset, units = run
    shape = (replicas, rows, units + sum(p.shape[1] for p in columns[:1]))
    return pl.pallas_call(
        mix_kernel,
        out_shape=jax.ShapeDtypeStruct(shape, kind),
        grid_spec=pltpu.PrefetchScalarGridSpec(
            num_scalar_prefetch=1,
            grid=(units // unit,),
            in_specs=[
                pl.BlockSpec(tokens.shape, lambda i, position: (0, 0, 0, 0)),
                pl.BlockSpec(
                    (unit, block),
                    lambda i, position: (position[0] * (quarter // unit) + offset // unit + i, 0),
                ),
                pl.BlockSpec((unit, block), lambda i, position: (i, 0)),
            ]
            + [pl.BlockSpec(p.shape, lambda i, position: (0, 0)) for p in columns],
            out_specs=pl.BlockSpec(shape, lambda i, position: (0, 0, 0)),
        ),
        compiler_params=pltpu.CompilerParams(vmem_limit_bytes=60 * 1024 * 1024),
        cost_estimate=pl.CostEstimate(flops=cost, bytes_accessed=0, transcendentals=0),
        name="hidden_grad_chunk",
    )(position, tokens, weight, cross, *columns)


def join_kernel(widths, *refs):
    count = len(widths)
    for d, out, at_row in ((0, refs[-3], 0), (1, refs[-2], 0), (2, refs[-1], 0), (3, refs[-1], 1)):

        @pl.when(pl.program_id(0) == d)
        def _():
            at = 0
            for width, kept, part in zip(widths, refs[:count], refs[count:-3]):
                total = kept[0, :, :width] + part[0, :, :width].astype(jnp.float32)
                out[at_row, :, at : at + width] = total.astype(out.dtype)
                at += width


def join(widths, kept, parts):
    replicas, rows, _ = kept[0].shape
    shapes = [(count, rows, sum(widths)) for count in (1, 1, 2)]
    return pl.pallas_call(
        functools.partial(join_kernel, widths),
        out_shape=[jax.ShapeDtypeStruct(shape, jnp.bfloat16) for shape in shapes],
        grid=(replicas,),
        in_specs=[
            pl.BlockSpec((1, rows, x.shape[2]), lambda i: (i, 0, 0)) for x in (*kept, *parts)
        ],
        out_specs=[pl.BlockSpec(shape, lambda i: (0, 0, 0)) for shape in shapes],
        compiler_params=pltpu.CompilerParams(vmem_limit_bytes=VMEM_BYTES),
        cost_estimate=LIGHT,
        name="hidden_grad_sum",
    )(*kept, *parts)


def grads_kernel(position, p0, p1, p2, p3, gate, up, *refs):
    grad_gate, grad_up = refs[-2:]
    for d, piece in enumerate((p0, p1, p2, p3)):

        @pl.when(pl.program_id(0) == d)
        def _():
            gate_float = gate[...].astype(jnp.float32)
            up_float = up[...].astype(jnp.float32)
            hidden_grad = piece[0].astype(jnp.float32)
            sigma = jax.nn.sigmoid(gate_float)
            grad_up[...] = (hidden_grad * (gate_float * sigma)).astype(grad_up.dtype)
            grad_gate[...] = (
                hidden_grad * up_float * sigma * (1.0 + gate_float * (1.0 - sigma))
            ).astype(grad_gate.dtype)


def grads(position, pieces, gate, up, kept, offset, quarter, unit):
    _, rows, width = pieces[0][0].shape
    subs = width // unit

    def piece_map(d):
        which = pieces[d][1]
        return lambda i, j, position: (
            which,
            0,
            jnp.where(i == d, j, jnp.where(i < d, 0, subs - 1)),
        )

    def column_map(i, j, position):
        return (0, (position[0] ^ i) * (quarter // unit) + offset // unit + j)

    columns = pl.BlockSpec((rows, unit), column_map)
    anywhere = pl.BlockSpec(memory_space=pl.ANY)
    return pl.pallas_call(
        grads_kernel,
        out_shape=[jax.ShapeDtypeStruct(gate.shape, jnp.bfloat16)] * 2,
        grid_spec=pltpu.PrefetchScalarGridSpec(
            num_scalar_prefetch=1,
            grid=(4, subs),
            in_specs=[pl.BlockSpec((1, rows, unit), piece_map(d)) for d in range(4)]
            + [columns, columns]
            + [anywhere] * len(kept),
            out_specs=[columns, columns],
        ),
        input_output_aliases={7: 0, 8: 1} if kept else {},
        compiler_params=pltpu.CompilerParams(vmem_limit_bytes=VMEM_BYTES),
        cost_estimate=pl.CostEstimate(
            flops=0, bytes_accessed=4 * 10 * rows * width, transcendentals=0
        ),
        name="grads_chunk",
    )(position, *(x for x, _ in pieces), gate, up, *kept)


def hidden_kernel(position, gate, up, *outs):
    gate_float = gate[...].astype(jnp.float32)
    activated = gate_float * jax.nn.sigmoid(gate_float)
    hidden = (activated * up[...].astype(jnp.float32)).astype(jnp.bfloat16)
    for d, out in enumerate(outs):

        @pl.when(pl.program_id(0) == d)
        def _():
            out[...] = hidden


def hidden_quarters(position, gate, up, quarter):
    rows = gate.shape[0]
    columns = pl.BlockSpec((rows, quarter), lambda i, position: (0, position[0] ^ i))
    return pl.pallas_call(
        hidden_kernel,
        out_shape=[jax.ShapeDtypeStruct((rows, quarter), jnp.bfloat16)] * 4,
        grid_spec=pltpu.PrefetchScalarGridSpec(
            num_scalar_prefetch=1,
            grid=(4,),
            in_specs=[columns, columns],
            out_specs=[pl.BlockSpec((rows, quarter), lambda i, position: (0, 0))] * 4,
        ),
        compiler_params=pltpu.CompilerParams(vmem_limit_bytes=VMEM_BYTES),
        cost_estimate=LIGHT,
        name="hidden_quarters",
    )(position, gate, up)


def terms_kernel(position, *refs):
    lows, hidden, (out, low) = refs[:4], refs[4:8], refs[8:]
    rows, width = lows[0].shape[1:]

    @pl.when(pl.program_id(0) == 0)
    def _():
        for e, piece in enumerate(lows):
            at = pl.multiple_of((position[0] ^ e) * width, width)
            for d in range(4):
                low[d * rows : (d + 1) * rows, pl.ds(at, width)] = piece[d ^ e]

    total = None
    for d, block in enumerate(hidden):
        term = lax.dot_general(
            low[d * rows : (d + 1) * rows, :],
            block[...],
            (((0,), (0,)), ((), ())),
            preferred_element_type=jnp.float32,
        )
        total = term if total is None else total + term
    out[...] = total


def rank_terms(position, lows, hidden):
    rows, quarter = hidden[0].shape
    rank = 4 * lows[0].shape[2]
    parts = 2 if quarter % 256 == 0 else 1
    width = quarter // parts
    return pl.pallas_call(
        terms_kernel,
        out_shape=jax.ShapeDtypeStruct((rank, quarter), jnp.float32),
        grid_spec=pltpu.PrefetchScalarGridSpec(
            num_scalar_prefetch=1,
            grid=(parts,),
            in_specs=[pl.BlockSpec(lows[0].shape, lambda i, position: (0, 0, 0))] * 4
            + [pl.BlockSpec((rows, width), lambda i, position: (0, i))] * 4,
            out_specs=pl.BlockSpec((rank, width), lambda i, position: (0, i)),
            scratch_shapes=[pltpu.VMEM((4 * rows, rank), jnp.bfloat16)],
        ),
        compiler_params=pltpu.CompilerParams(vmem_limit_bytes=VMEM_BYTES),
        cost_estimate=LIGHT,
        name="rank_terms",
    )(position, *lows, *hidden)


def widen_kernel(position, *refs):
    for d, piece in enumerate(refs[:-1]):

        @pl.when(pl.program_id(0) == d)
        def _():
            refs[-1][...] = piece[0].astype(refs[-1].dtype)


def widen(position, pieces):
    _, rows, quarter = pieces[0][0].shape
    return pl.pallas_call(
        widen_kernel,
        out_shape=jax.ShapeDtypeStruct((rows, len(pieces) * quarter), jnp.float32),
        grid_spec=pltpu.PrefetchScalarGridSpec(
            num_scalar_prefetch=1,
            grid=(len(pieces),),
            in_specs=[
                pl.BlockSpec((1, rows, quarter), lambda i, position, which=which: (which, 0, 0))
                for _, which in pieces
            ],
            out_specs=pl.BlockSpec((rows, quarter), lambda i, position: (0, position[0] ^ i)),
        ),
        compiler_params=pltpu.CompilerParams(vmem_limit_bytes=VMEM_BYTES),
        cost_estimate=LIGHT,
        name="projected_grad",
    )(position, *(x for x, _ in pieces))


def line(cotangent, gate_pre, up_pre, down_weight, projector):
    replicas, shards, tensors = (lax.axis_size(a) for a in AXES)
    r, f, t = (lax.axis_index(a) for a in AXES)
    rows = cotangent.shape[0]
    quarter = down_weight.shape[0] // replicas
    block = down_weight.shape[1]
    bf16, f32 = jnp.bfloat16, jnp.float32

    def send(x, move, sends=lambda a, b, c: True):
        pairs = []
        for a in range(replicas):
            for b in range(shards):
                for c in range(tensors):
                    here = (a * shards + b) * tensors + c
                    there = ((a ^ move[0]) * shards + (b ^ move[1])) * tensors + (c ^ move[2])
                    if sends(a, b, c):
                        pairs.append((here, there))
        return lax.ppermute(x, AXES, pairs)

    def after(x, *earlier):
        return lax.optimization_barrier((x, *earlier))[0]

    along, beyond, over_tensor = (0, 1, 0), (0, 2, 0), (0, 0, 1)
    odd, high = f % 2, f // 2
    position = jnp.stack([r, high]).astype(jnp.int32)
    unit = 256 if quarter % 256 == 0 else 128
    plan = chunk_plan(quarter, unit, 4)

    def total_of(first, kept, parts):
        return join([plan[first + i][1] for i in range(len(kept))], kept, parts)

    def over_replicas(total, *earlier):
        return send(after(total[2], *earlier), (2, 0, 0))

    def over_cores(total, arrived, *earlier):
        x = jnp.concatenate([total[1], arrived[1:]], axis=0)
        return send(after(x, *earlier), (1, 0, 0))

    def finish(k, total, arrived, last, written):
        pieces = [(total[0], 0), (last, 0), (arrived, 0), (last, 1)]
        return grads(position, pieces, gate_pre, up_pre, written, plan[k][0], quarter, unit)

    own_rows = [
        lax.dynamic_slice_in_dim(down_weight, r * quarter + offset, count, 0)
        for offset, count in plan
    ]

    def chunk(k, tokens, kind, columns=(), cost=0):
        return mix(
            position, tokens, down_weight, quarter, plan[k], unit, cross[k], columns, kind, cost
        )

    mine = lax.dynamic_slice_in_dim(cotangent, odd * block, block, 1)
    give = lax.dynamic_slice_in_dim(cotangent, (1 - odd) * block, block, 1)
    given = send(give, along)
    halves = [projector[:block], projector[block:]]
    found = jnp.where(odd == 0, halves[0], halves[1])
    for d in (1, 2, 3):
        x = jnp.where((odd == 0) == (d == 2), halves[0], halves[1])
        column = send(x, (0, d, 0), lambda a, b, c: a == b)
        found = jnp.where(r ^ f == d, column, found)
    def everyone(x):
        return lax.all_gather(x, ("replica", "tensor")).reshape((replicas, tensors) + x.shape)

    theirs_all = everyone(after(given, found))
    mine_all = everyone(after(mine, given, found))
    hidden = hidden_quarters(position, gate_pre, up_pre, quarter)
    tick = (given, found)
    light, heavy = 0, 16 * rows * block * plan[0][1]

    cross = [send(after(own_rows[0], *tick), beyond)]
    theirs = send(after(found, *tick), over_tensor)
    columns = [jnp.where(t == 0, found, theirs), jnp.where(t == 0, theirs, found)]
    met = {1: send(after(hidden[1], *tick), (1, 0, 0))}
    sent = [chunk(0, after(theirs_all, *tick), bf16, columns, heavy)]
    tick = (sent[0], met[1])

    cross.append(send(after(own_rows[1], *tick), beyond))
    parts = [send(after(sent[0], *tick), along)]
    met[2] = send(after(hidden[2], *tick), (2, 0, 0))
    met[3] = send(after(hidden[3], *tick), (3, 0, 0))
    kept = [chunk(0, after(mine_all, *tick), f32, columns, light)]
    sent.append(chunk(1, after(theirs_all, *tick), bf16, (), heavy))
    tick = (sent[1], parts[0], met[2], met[3], kept[0])

    cross.append(send(after(own_rows[2], *tick), beyond))
    parts.append(send(after(sent[1], *tick), along))
    width = plan[0][1]
    low = (kept[0][:, :, width:] + after(parts[0], *tick)[:, :, width:].astype(f32)).astype(bf16)
    lows = [low] + [send(low, (d, 0, 0)) for d in (1, 2, 3)]
    kept.append(chunk(1, after(mine_all, *tick), f32, (), light))
    total = rank_terms(position, after(lows, kept[1]), [hidden[0], met[1], met[2], met[3]])
    piece = 4 * low.shape[2] // shards
    total = total.reshape(2, 2, piece, quarter)
    theirs = jnp.where(odd == 0, total[:, 1], total[:, 0]).astype(bf16)
    total = jnp.where(odd == 0, total[:, 0], total[:, 1])
    sent.append(chunk(2, after(theirs_all, *tick), bf16, (), heavy))
    tick = (sent[2], theirs, parts[1])

    cross.append(send(after(own_rows[3], *tick), beyond))
    stage = send(after(theirs, *tick), along)
    parts.append(send(after(sent[2], *tick), along))
    first = total_of(0, after(kept, *tick), parts[:2])
    first_y = over_replicas(first)
    kept.append(chunk(2, after(mine_all, *tick), f32, (), light))
    sent.append(chunk(3, after(theirs_all, *tick), bf16, (), 8 * heavy))
    total = total + after(stage, sent[3]).astype(f32)
    theirs = jnp.where(high == 0, total[1], total[0]).astype(bf16)
    total = jnp.where(high == 0, total[0], total[1])
    tick = (theirs, kept[2], parts[2], first_y)

    crossed = send(after(theirs, *tick), beyond)
    parts.append(send(after(sent[3], *tick), along))
    first_home = over_cores(first, first_y, *tick)
    second = total_of(2, after(kept[2:], *tick), parts[2:3])
    second_y = over_replicas(second)
    kept.append(chunk(3, after(mine_all, *tick), f32, (), light))
    scale_factor = 1.0 / math.sqrt(rows * replicas * shards)
    final = ((total + crossed.astype(f32)) * scale_factor).astype(bf16)
    tick = (final, parts[3], kept[3], first_home, second_y)

    over_y = send(after(final, *tick), (2, 0, 0))
    second_home = over_cores(second, second_y, *tick)
    third = total_of(3, after(kept[3:], *tick), parts[3:])
    third_y = over_replicas(third)
    written = finish(0, first, first_y, first_home, ())
    tick = (over_y, second_home, third_y, written[0])

    two = jnp.stack([final, over_y])
    other = send(after(two, *tick), (1, 0, 0))
    third_home = over_cores(third, third_y, *tick)
    written = finish(2, second, second_y, second_home, after(written, *tick))
    kept = finish(3, third, third_y, third_home, written)
    projected_grad = widen(position, ((two, 0), (other, 0), (two, 1), (other, 1)))
    return (kept[0], kept[1], projected_grad)


def solution(mesh):
    sizes = tuple(mesh.shape[a] for a in AXES)
    placed = (
        P(("replica", "fsdp"), "tensor"),
        P(("replica", "fsdp"), "tensor"),
        P(("replica", "fsdp"), "tensor"),
        P("tensor", "fsdp"),
        P("tensor", "fsdp"),
    )
    return jax.shard_map(
        line if sizes == (4, 4, 2) else general,
        mesh=mesh,
        in_specs=placed,
        out_specs=(
            P(("replica", "fsdp"), "tensor"),
            P(("replica", "fsdp"), "tensor"),
            P("fsdp", "tensor"),
        ),
        check_vma=False,
    )
```

```python
import functools
import math

import jax
import jax.numpy as jnp
from jax import lax
from jax.experimental import pallas as pl
from jax.experimental.pallas import tpu as pltpu
from jax.sharding import PartitionSpec as P

AXES = ("replica", "fsdp", "tensor")
VMEM_BYTES = 24 * 1024 * 1024
LIGHT = pl.CostEstimate(flops=0, bytes_accessed=0, transcendentals=0)


def general(cotangent, gate_pre, up_pre, down_weight, projector):
    whole = lax.all_gather(cotangent, "tensor", axis=1, tiled=True)
    local_rows = cotangent.shape[0]
    hidden_cols = gate_pre.shape[1]
    hidden_grad = lax.dot_general(
        whole,
        lax.all_gather(down_weight, "fsdp", axis=1, tiled=True),
        (((1,), (1,)), ((), ())),
        preferred_element_type=jnp.float32,
    )
    projector_full_cols = lax.all_gather(projector, "fsdp", axis=1, tiled=True)
    partial_rank = jnp.dot(cotangent, projector_full_cols, preferred_element_type=jnp.float32)
    low_rank = lax.psum(partial_rank, "tensor").astype(jnp.bfloat16)
    gate_float = gate_pre.astype(jnp.float32)
    up_float = up_pre.astype(jnp.float32)
    sigma = jax.nn.sigmoid(gate_float)
    activated = gate_float * sigma
    hidden = (activated * up_float).astype(jnp.bfloat16)
    grad_up = (hidden_grad * activated).astype(jnp.bfloat16)
    grad_gate = (hidden_grad * up_float * sigma * (1.0 + gate_float * (1.0 - sigma))).astype(
        jnp.bfloat16
    )
    replicas = lax.axis_size("replica")
    shards = lax.axis_size("fsdp")
    token_total = local_rows * replicas * shards
    scale_factor = 1.0 / math.sqrt(token_total)
    partial_grad = (
        lax.dot_general(
            low_rank, hidden, (((0,), (0,)), ((), ())), preferred_element_type=jnp.float32
        )
        * scale_factor
    )
    rank_size = partial_grad.shape[0]
    piece_rows = rank_size // (shards * replicas)
    reordered = partial_grad.reshape(shards, replicas, piece_rows, hidden_cols)
    reordered = jnp.swapaxes(reordered, 0, 1).reshape(rank_size, hidden_cols)
    joint_piece = lax.psum_scatter(reordered, ("replica", "fsdp"), scatter_dimension=0, tiled=True)
    projected_grad = lax.all_gather(joint_piece, "replica", axis=0, tiled=True)
    return (grad_gate, grad_up, projected_grad)


def chunk_plan(quarter, unit, count):
    units = quarter // unit
    each = -(-units // count)
    plan, at = [], 0
    while at < units:
        width = min(each, units - at)
        plan.append((at * unit, width * unit))
        at += width
    return plan


def mix_kernel(position, tokens, own, cross, *refs):
    columns, out = refs[:-1], refs[-1]
    replicas, _, rows, block = tokens.shape
    at = position[1]
    unit = own.shape[0]
    step = pl.program_id(0)
    where = pl.ds(pl.multiple_of(step * unit, unit), unit)
    total = None
    for side, w in ((at, own[...]), (1 - at, cross[...])):
        x = tokens[:, side].reshape(replicas * rows, block)
        term = lax.dot_general(
            x, w, (((1,), (1,)), ((), ())), preferred_element_type=jnp.float32
        )
        total = term if total is None else total + term
    for a in range(replicas):
        out[position[0] ^ a, :, where] = total[a * rows : (a + 1) * rows].astype(out.dtype)
    if columns:
        width = columns[0].shape[1]

        @pl.when(step == 0)
        def _():
            total = None
            for side, p in enumerate(columns):
                x = tokens[:, side].reshape(replicas * rows, block)
                term = jnp.dot(x, p[...], preferred_element_type=jnp.float32)
                total = term if total is None else total + term
            for a in range(replicas):
                out[position[0] ^ a, :, out.shape[2] - width :] = total[
                    a * rows : (a + 1) * rows
                ].astype(out.dtype)


def mix(position, tokens, weight, quarter, run, unit, cross, columns, kind, cost):
    replicas, _, rows, _ = tokens.shape
    block = weight.shape[1]
    offset, units = run
    shape = (replicas, rows, units + sum(p.shape[1] for p in columns[:1]))
    return pl.pallas_call(
        mix_kernel,
        out_shape=jax.ShapeDtypeStruct(shape, kind),
        grid_spec=pltpu.PrefetchScalarGridSpec(
            num_scalar_prefetch=1,
            grid=(units // unit,),
            in_specs=[
                pl.BlockSpec(tokens.shape, lambda i, position: (0, 0, 0, 0)),
                pl.BlockSpec(
                    (unit, block),
                    lambda i, position: (position[0] * (quarter // unit) + offset // unit + i, 0),
                ),
                pl.BlockSpec((unit, block), lambda i, position: (i, 0)),
            ]
            + [pl.BlockSpec(p.shape, lambda i, position: (0, 0)) for p in columns],
            out_specs=pl.BlockSpec(shape, lambda i, position: (0, 0, 0)),
        ),
        compiler_params=pltpu.CompilerParams(vmem_limit_bytes=VMEM_BYTES),
        cost_estimate=pl.CostEstimate(flops=cost, bytes_accessed=0, transcendentals=0),
        name="hidden_grad_chunk",
    )(position, tokens, weight, cross, *columns)


def join_kernel(widths, *refs):
    count = len(widths)
    for d, out, at_row in ((0, refs[-3], 0), (1, refs[-2], 0), (2, refs[-1], 0), (3, refs[-1], 1)):

        @pl.when(pl.program_id(0) == d)
        def _():
            at = 0
            for width, kept, part in zip(widths, refs[:count], refs[count:-3]):
                total = kept[0, :, :width] + part[0, :, :width].astype(jnp.float32)
                out[at_row, :, at : at + width] = total.astype(out.dtype)
                at += width


def join(widths, kept, parts):
    replicas, rows, _ = kept[0].shape
    shapes = [(count, rows, sum(widths)) for count in (1, 1, 2)]
    return pl.pallas_call(
        functools.partial(join_kernel, widths),
        out_shape=[jax.ShapeDtypeStruct(shape, jnp.bfloat16) for shape in shapes],
        grid=(replicas,),
        in_specs=[
            pl.BlockSpec((1, rows, x.shape[2]), lambda i: (i, 0, 0)) for x in (*kept, *parts)
        ],
        out_specs=[pl.BlockSpec(shape, lambda i: (0, 0, 0)) for shape in shapes],
        compiler_params=pltpu.CompilerParams(vmem_limit_bytes=VMEM_BYTES),
        cost_estimate=LIGHT,
        name="hidden_grad_sum",
    )(*kept, *parts)


def grads_kernel(position, p0, p1, p2, p3, gate, up, *refs):
    grad_gate, grad_up = refs[-2:]
    for d, piece in enumerate((p0, p1, p2, p3)):

        @pl.when(pl.program_id(0) == d)
        def _():
            gate_float = gate[...].astype(jnp.float32)
            up_float = up[...].astype(jnp.float32)
            hidden_grad = piece[0].astype(jnp.float32)
            sigma = jax.nn.sigmoid(gate_float)
            grad_up[...] = (hidden_grad * (gate_float * sigma)).astype(grad_up.dtype)
            grad_gate[...] = (
                hidden_grad * up_float * sigma * (1.0 + gate_float * (1.0 - sigma))
            ).astype(grad_gate.dtype)


def grads(position, pieces, gate, up, kept, offset, quarter, unit):
    _, rows, width = pieces[0][0].shape
    subs = width // unit

    def piece_map(d):
        which = pieces[d][1]
        return lambda i, j, position: (
            which,
            0,
            jnp.where(i == d, j, jnp.where(i < d, 0, subs - 1)),
        )

    def column_map(i, j, position):
        return (0, (position[0] ^ i) * (quarter // unit) + offset // unit + j)

    columns = pl.BlockSpec((rows, unit), column_map)
    anywhere = pl.BlockSpec(memory_space=pl.ANY)
    return pl.pallas_call(
        grads_kernel,
        out_shape=[jax.ShapeDtypeStruct(gate.shape, jnp.bfloat16)] * 2,
        grid_spec=pltpu.PrefetchScalarGridSpec(
            num_scalar_prefetch=1,
            grid=(4, subs),
            in_specs=[pl.BlockSpec((1, rows, unit), piece_map(d)) for d in range(4)]
            + [columns, columns]
            + [anywhere] * len(kept),
            out_specs=[columns, columns],
        ),
        input_output_aliases={7: 0, 8: 1} if kept else {},
        compiler_params=pltpu.CompilerParams(vmem_limit_bytes=VMEM_BYTES),
        cost_estimate=pl.CostEstimate(
            flops=0, bytes_accessed=4 * 10 * rows * width, transcendentals=0
        ),
        name="grads_chunk",
    )(position, *(x for x, _ in pieces), gate, up, *kept)


def hidden_kernel(position, gate, up, *outs):
    gate_float = gate[...].astype(jnp.float32)
    activated = gate_float * jax.nn.sigmoid(gate_float)
    hidden = (activated * up[...].astype(jnp.float32)).astype(jnp.bfloat16)
    for d, out in enumerate(outs):

        @pl.when(pl.program_id(0) == d)
        def _():
            out[...] = hidden


def hidden_quarters(position, gate, up, quarter):
    rows = gate.shape[0]
    columns = pl.BlockSpec((rows, quarter), lambda i, position: (0, position[0] ^ i))
    return pl.pallas_call(
        hidden_kernel,
        out_shape=[jax.ShapeDtypeStruct((rows, quarter), jnp.bfloat16)] * 4,
        grid_spec=pltpu.PrefetchScalarGridSpec(
            num_scalar_prefetch=1,
            grid=(4,),
            in_specs=[columns, columns],
            out_specs=[pl.BlockSpec((rows, quarter), lambda i, position: (0, 0))] * 4,
        ),
        compiler_params=pltpu.CompilerParams(vmem_limit_bytes=VMEM_BYTES),
        cost_estimate=LIGHT,
        name="hidden_quarters",
    )(position, gate, up)


def terms_kernel(position, *refs):
    lows, hidden, (out, low) = refs[:4], refs[4:8], refs[8:]
    rows, width = lows[0].shape[1:]

    @pl.when(pl.program_id(0) == 0)
    def _():
        for e, piece in enumerate(lows):
            at = pl.multiple_of((position[0] ^ e) * width, width)
            for d in range(4):
                low[d * rows : (d + 1) * rows, pl.ds(at, width)] = piece[d ^ e]

    total = None
    for d, block in enumerate(hidden):
        term = lax.dot_general(
            low[d * rows : (d + 1) * rows, :],
            block[...],
            (((0,), (0,)), ((), ())),
            preferred_element_type=jnp.float32,
        )
        total = term if total is None else total + term
    out[...] = total


def rank_terms(position, lows, hidden):
    rows, quarter = hidden[0].shape
    rank = 4 * lows[0].shape[2]
    parts = 2 if quarter % 256 == 0 else 1
    width = quarter // parts
    return pl.pallas_call(
        terms_kernel,
        out_shape=jax.ShapeDtypeStruct((rank, quarter), jnp.float32),
        grid_spec=pltpu.PrefetchScalarGridSpec(
            num_scalar_prefetch=1,
            grid=(parts,),
            in_specs=[pl.BlockSpec(lows[0].shape, lambda i, position: (0, 0, 0))] * 4
            + [pl.BlockSpec((rows, width), lambda i, position: (0, i))] * 4,
            out_specs=pl.BlockSpec((rank, width), lambda i, position: (0, i)),
            scratch_shapes=[pltpu.VMEM((4 * rows, rank), jnp.bfloat16)],
        ),
        compiler_params=pltpu.CompilerParams(vmem_limit_bytes=VMEM_BYTES),
        cost_estimate=LIGHT,
        name="rank_terms",
    )(position, *lows, *hidden)


def widen_kernel(position, *refs):
    for d, piece in enumerate(refs[:-1]):

        @pl.when(pl.program_id(0) == d)
        def _():
            refs[-1][...] = piece[0].astype(refs[-1].dtype)


def widen(position, pieces):
    _, rows, quarter = pieces[0][0].shape
    return pl.pallas_call(
        widen_kernel,
        out_shape=jax.ShapeDtypeStruct((rows, len(pieces) * quarter), jnp.float32),
        grid_spec=pltpu.PrefetchScalarGridSpec(
            num_scalar_prefetch=1,
            grid=(len(pieces),),
            in_specs=[
                pl.BlockSpec((1, rows, quarter), lambda i, position, which=which: (which, 0, 0))
                for _, which in pieces
            ],
            out_specs=pl.BlockSpec((rows, quarter), lambda i, position: (0, position[0] ^ i)),
        ),
        compiler_params=pltpu.CompilerParams(vmem_limit_bytes=VMEM_BYTES),
        cost_estimate=LIGHT,
        name="projected_grad",
    )(position, *(x for x, _ in pieces))


def line(cotangent, gate_pre, up_pre, down_weight, projector):
    replicas, shards, tensors = (lax.axis_size(a) for a in AXES)
    r, f, t = (lax.axis_index(a) for a in AXES)
    rows = cotangent.shape[0]
    quarter = down_weight.shape[0] // replicas
    block = down_weight.shape[1]
    bf16, f32 = jnp.bfloat16, jnp.float32

    def send(x, move, sends=lambda a, b, c: True):
        pairs = []
        for a in range(replicas):
            for b in range(shards):
                for c in range(tensors):
                    here = (a * shards + b) * tensors + c
                    there = ((a ^ move[0]) * shards + (b ^ move[1])) * tensors + (c ^ move[2])
                    if sends(a, b, c):
                        pairs.append((here, there))
        return lax.ppermute(x, AXES, pairs)

    def after(x, *earlier):
        return lax.optimization_barrier((x, *earlier))[0]

    along, beyond, over_tensor = (0, 1, 0), (0, 2, 0), (0, 0, 1)
    odd, high = f % 2, f // 2
    position = jnp.stack([r, high]).astype(jnp.int32)
    unit = 256 if quarter % 256 == 0 else 128
    plan = chunk_plan(quarter, unit, 4)

    def total_of(first, kept, parts):
        return join([plan[first + i][1] for i in range(len(kept))], kept, parts)

    def over_replicas(total, *earlier):
        return send(after(total[2], *earlier), (2, 0, 0))

    def over_cores(total, arrived, *earlier):
        x = jnp.concatenate([total[1], arrived[1:]], axis=0)
        return send(after(x, *earlier), (1, 0, 0))

    def finish(k, total, arrived, last, written):
        pieces = [(total[0], 0), (last, 0), (arrived, 0), (last, 1)]
        return grads(position, pieces, gate_pre, up_pre, written, plan[k][0], quarter, unit)

    own_rows = [
        lax.dynamic_slice_in_dim(down_weight, r * quarter + offset, count, 0)
        for offset, count in plan
    ]

    def chunk(k, tokens, kind, columns=(), cost=0):
        return mix(
            position, tokens, down_weight, quarter, plan[k], unit, cross[k], columns, kind, cost
        )

    mine = lax.dynamic_slice_in_dim(cotangent, odd * block, block, 1)
    give = lax.dynamic_slice_in_dim(cotangent, (1 - odd) * block, block, 1)
    given = send(give, along)
    halves = [projector[:block], projector[block:]]
    found = jnp.where(odd == 0, halves[0], halves[1])
    for d in (1, 2, 3):
        x = jnp.where((odd == 0) == (d == 2), halves[0], halves[1])
        column = send(x, (0, d, 0), lambda a, b, c: a == b)
        found = jnp.where(r ^ f == d, column, found)
    def everyone(x):
        return lax.all_gather(x, ("replica", "tensor")).reshape((replicas, tensors) + x.shape)

    theirs_all = everyone(after(given, found))
    mine_all = everyone(after(mine, given, found))
    hidden = hidden_quarters(position, gate_pre, up_pre, quarter)
    tick = (given, found)
    light, heavy = 0, 16 * rows * block * plan[0][1]

    cross = [send(after(own_rows[0], *tick), beyond)]
    theirs = send(after(found, *tick), over_tensor)
    columns = [jnp.where(t == 0, found, theirs), jnp.where(t == 0, theirs, found)]
    met = {1: send(after(hidden[1], *tick), (1, 0, 0))}
    sent = [chunk(0, after(theirs_all, met[1]), bf16, columns, heavy)]
    tick = (sent[0], met[1])

    cross.append(send(after(own_rows[1], cross[0], theirs_all, *columns, met[1]), beyond))
    parts = [send(after(sent[0], *tick), along)]
    met[2] = send(after(hidden[2], *tick), (2, 0, 0))
    met[3] = send(after(hidden[3], *tick), (3, 0, 0))
    kept = [chunk(0, after(mine_all, *tick), f32, columns, light)]
    sent.append(chunk(1, after(theirs_all, *tick), bf16, (), 2 * heavy))
    tick = (sent[1], parts[0], met[2], met[3], kept[0])

    cross.append(send(after(own_rows[2], cross[1], *tick[1:]), beyond))
    parts.append(send(after(sent[1], *tick), along))
    width = plan[0][1]
    low = (kept[0][:, :, width:] + after(parts[0], *tick)[:, :, width:].astype(f32)).astype(bf16)
    lows = [low] + [send(low, (d, 0, 0)) for d in (1, 2, 3)]
    kept.append(chunk(1, after(mine_all, *tick), f32, (), light))
    total = rank_terms(position, after(lows, kept[1]), [hidden[0], met[1], met[2], met[3]])
    piece = 4 * low.shape[2] // shards
    total = total.reshape(2, 2, piece, quarter)
    theirs = jnp.where(odd == 0, total[:, 1], total[:, 0]).astype(bf16)
    total = jnp.where(odd == 0, total[:, 0], total[:, 1])
    sent.append(chunk(2, after(theirs_all, *tick), bf16, (), 3 * heavy))
    tick = (sent[2], theirs, parts[1])

    cross.append(send(after(own_rows[3], cross[2], *tick[1:]), beyond))
    stage = send(after(theirs, *tick), along)
    parts.append(send(after(sent[2], *tick), along))
    first = total_of(0, after(kept, *tick), parts[:2])
    first_y = over_replicas(first)
    kept.append(chunk(2, after(mine_all, *tick), f32, (), light))
    sent.append(chunk(3, after(theirs_all, *tick), bf16, (), 8 * heavy))
    total = total + after(stage, sent[3]).astype(f32)
    theirs = jnp.where(high == 0, total[1], total[0]).astype(bf16)
    total = jnp.where(high == 0, total[0], total[1])
    tick = (theirs, kept[2], parts[2], first_y)

    crossed = send(after(theirs, *tick), beyond)
    parts.append(send(after(sent[3], *tick), along))
    first_home = over_cores(first, first_y, *tick)
    second = total_of(2, after(kept[2:], *tick), parts[2:3])
    second_y = over_replicas(second)
    kept.append(chunk(3, after(mine_all, *tick), f32, (), light))
    scale_factor = 1.0 / math.sqrt(rows * replicas * shards)
    final = ((total + crossed.astype(f32)) * scale_factor).astype(bf16)
    tick = (final, parts[3], kept[3], first_home, second_y)

    over_y = send(after(final, *tick), (2, 0, 0))
    second_home = over_cores(second, second_y, *tick)
    third = total_of(3, after(kept[3:], *tick), parts[3:])
    third_y = over_replicas(third)
    written = finish(0, first, first_y, first_home, ())
    tick = (over_y, second_home, third_y, written[0])

    two = jnp.stack([final, over_y])
    other = send(after(two, *tick), (1, 0, 0))
    third_home = over_cores(third, third_y, *tick)
    written = finish(2, second, second_y, second_home, after(written, *tick))
    kept = finish(3, third, third_y, third_home, written)
    projected_grad = widen(position, ((two, 0), (other, 0), (two, 1), (other, 1)))
    return (kept[0], kept[1], projected_grad)


def solution(mesh):
    sizes = tuple(mesh.shape[a] for a in AXES)
    placed = (
        P(("replica", "fsdp"), "tensor"),
        P(("replica", "fsdp"), "tensor"),
        P(("replica", "fsdp"), "tensor"),
        P("tensor", "fsdp"),
        P("tensor", "fsdp"),
    )
    return jax.shard_map(
        line if sizes == (4, 4, 2) else general,
        mesh=mesh,
        in_specs=placed,
        out_specs=(
            P(("replica", "fsdp"), "tensor"),
            P(("replica", "fsdp"), "tensor"),
            P("fsdp", "tensor"),
        ),
        check_vma=False,
    )
```

```python
import functools
import math

import jax
import jax.numpy as jnp
from jax import lax
from jax.experimental import pallas as pl
from jax.experimental.pallas import tpu as pltpu
from jax.sharding import PartitionSpec as P

AXES = ("replica", "fsdp", "tensor")
VMEM_BYTES = 24 * 1024 * 1024
LIGHT = pl.CostEstimate(flops=0, bytes_accessed=0, transcendentals=0)


def general(cotangent, gate_pre, up_pre, down_weight, projector):
    whole = lax.all_gather(cotangent, "tensor", axis=1, tiled=True)
    local_rows = cotangent.shape[0]
    hidden_cols = gate_pre.shape[1]
    hidden_grad = lax.dot_general(
        whole,
        lax.all_gather(down_weight, "fsdp", axis=1, tiled=True),
        (((1,), (1,)), ((), ())),
        preferred_element_type=jnp.float32,
    )
    projector_full_cols = lax.all_gather(projector, "fsdp", axis=1, tiled=True)
    partial_rank = jnp.dot(cotangent, projector_full_cols, preferred_element_type=jnp.float32)
    low_rank = lax.psum(partial_rank, "tensor").astype(jnp.bfloat16)
    gate_float = gate_pre.astype(jnp.float32)
    up_float = up_pre.astype(jnp.float32)
    sigma = jax.nn.sigmoid(gate_float)
    activated = gate_float * sigma
    hidden = (activated * up_float).astype(jnp.bfloat16)
    grad_up = (hidden_grad * activated).astype(jnp.bfloat16)
    grad_gate = (hidden_grad * up_float * sigma * (1.0 + gate_float * (1.0 - sigma))).astype(
        jnp.bfloat16
    )
    replicas = lax.axis_size("replica")
    shards = lax.axis_size("fsdp")
    token_total = local_rows * replicas * shards
    scale_factor = 1.0 / math.sqrt(token_total)
    partial_grad = (
        lax.dot_general(
            low_rank, hidden, (((0,), (0,)), ((), ())), preferred_element_type=jnp.float32
        )
        * scale_factor
    )
    rank_size = partial_grad.shape[0]
    piece_rows = rank_size // (shards * replicas)
    reordered = partial_grad.reshape(shards, replicas, piece_rows, hidden_cols)
    reordered = jnp.swapaxes(reordered, 0, 1).reshape(rank_size, hidden_cols)
    joint_piece = lax.psum_scatter(reordered, ("replica", "fsdp"), scatter_dimension=0, tiled=True)
    projected_grad = lax.all_gather(joint_piece, "replica", axis=0, tiled=True)
    return (grad_gate, grad_up, projected_grad)


def chunk_plan(quarter, unit, count):
    units = quarter // unit
    each = -(-units // count)
    plan, at = [], 0
    while at < units:
        width = min(each, units - at)
        plan.append((at * unit, width * unit))
        at += width
    return plan


def mix_kernel(position, tokens, own, cross, *refs):
    columns, out = refs[:-1], refs[-1]
    replicas, _, rows, block = tokens.shape
    at = position[1]
    unit = own.shape[0]
    step = pl.program_id(0)
    where = pl.ds(pl.multiple_of(step * unit, unit), unit)
    total = None
    for side, w in ((at, own[...]), (1 - at, cross[...])):
        x = tokens[:, side].reshape(replicas * rows, block)
        term = lax.dot_general(
            x, w, (((1,), (1,)), ((), ())), preferred_element_type=jnp.float32
        )
        total = term if total is None else total + term
    for a in range(replicas):
        out[position[0] ^ a, :, where] = total[a * rows : (a + 1) * rows].astype(out.dtype)
    if columns:
        width = columns[0].shape[1]

        @pl.when(step == 0)
        def _():
            total = None
            for side, p in enumerate(columns):
                x = tokens[:, side].reshape(replicas * rows, block)
                term = jnp.dot(x, p[...], preferred_element_type=jnp.float32)
                total = term if total is None else total + term
            for a in range(replicas):
                out[position[0] ^ a, :, out.shape[2] - width :] = total[
                    a * rows : (a + 1) * rows
                ].astype(out.dtype)


def mix(position, tokens, weight, quarter, run, unit, cross, columns, kind, cost):
    replicas, _, rows, _ = tokens.shape
    block = weight.shape[1]
    offset, units = run
    shape = (replicas, rows, units + sum(p.shape[1] for p in columns[:1]))
    return pl.pallas_call(
        mix_kernel,
        out_shape=jax.ShapeDtypeStruct(shape, kind),
        grid_spec=pltpu.PrefetchScalarGridSpec(
            num_scalar_prefetch=1,
            grid=(units // unit,),
            in_specs=[
                pl.BlockSpec(tokens.shape, lambda i, position: (0, 0, 0, 0)),
                pl.BlockSpec(
                    (unit, block),
                    lambda i, position: (position[0] * (quarter // unit) + offset // unit + i, 0),
                ),
                pl.BlockSpec((unit, block), lambda i, position: (i, 0)),
            ]
            + [pl.BlockSpec(p.shape, lambda i, position: (0, 0)) for p in columns],
            out_specs=pl.BlockSpec(shape, lambda i, position: (0, 0, 0)),
        ),
        compiler_params=pltpu.CompilerParams(vmem_limit_bytes=VMEM_BYTES),
        cost_estimate=pl.CostEstimate(flops=cost, bytes_accessed=0, transcendentals=0),
        name="hidden_grad_chunk",
    )(position, tokens, weight, cross, *columns)


def join_kernel(widths, *refs):
    count = len(widths)
    for d, out, at_row in ((0, refs[-3], 0), (1, refs[-2], 0), (2, refs[-1], 0), (3, refs[-1], 1)):

        @pl.when(pl.program_id(0) == d)
        def _():
            at = 0
            for width, kept, part in zip(widths, refs[:count], refs[count:-3]):
                total = kept[0, :, :width] + part[0, :, :width].astype(jnp.float32)
                out[at_row, :, at : at + width] = total.astype(out.dtype)
                at += width


def join(widths, kept, parts):
    replicas, rows, _ = kept[0].shape
    shapes = [(count, rows, sum(widths)) for count in (1, 1, 2)]
    return pl.pallas_call(
        functools.partial(join_kernel, widths),
        out_shape=[jax.ShapeDtypeStruct(shape, jnp.bfloat16) for shape in shapes],
        grid=(replicas,),
        in_specs=[
            pl.BlockSpec((1, rows, x.shape[2]), lambda i: (i, 0, 0)) for x in (*kept, *parts)
        ],
        out_specs=[pl.BlockSpec(shape, lambda i: (0, 0, 0)) for shape in shapes],
        compiler_params=pltpu.CompilerParams(vmem_limit_bytes=VMEM_BYTES),
        cost_estimate=LIGHT,
        name="hidden_grad_sum",
    )(*kept, *parts)


def grads_kernel(position, p0, p1, p2, p3, gate, up, *refs):
    grad_gate, grad_up = refs[-2:]
    for d, piece in enumerate((p0, p1, p2, p3)):

        @pl.when(pl.program_id(0) == d)
        def _():
            gate_float = gate[...].astype(jnp.float32)
            up_float = up[...].astype(jnp.float32)
            hidden_grad = piece[0].astype(jnp.float32)
            sigma = jax.nn.sigmoid(gate_float)
            grad_up[...] = (hidden_grad * (gate_float * sigma)).astype(grad_up.dtype)
            grad_gate[...] = (
                hidden_grad * up_float * sigma * (1.0 + gate_float * (1.0 - sigma))
            ).astype(grad_gate.dtype)


def grads(position, pieces, gate, up, kept, offset, quarter, unit):
    _, rows, width = pieces[0][0].shape
    subs = width // unit

    def piece_map(d):
        which = pieces[d][1]
        return lambda i, j, position: (
            which,
            0,
            jnp.where(i == d, j, jnp.where(i < d, 0, subs - 1)),
        )

    def column_map(i, j, position):
        return (0, (position[0] ^ i) * (quarter // unit) + offset // unit + j)

    columns = pl.BlockSpec((rows, unit), column_map)
    anywhere = pl.BlockSpec(memory_space=pl.ANY)
    return pl.pallas_call(
        grads_kernel,
        out_shape=[jax.ShapeDtypeStruct(gate.shape, jnp.bfloat16)] * 2,
        grid_spec=pltpu.PrefetchScalarGridSpec(
            num_scalar_prefetch=1,
            grid=(4, subs),
            in_specs=[pl.BlockSpec((1, rows, unit), piece_map(d)) for d in range(4)]
            + [columns, columns]
            + [anywhere] * len(kept),
            out_specs=[columns, columns],
        ),
        input_output_aliases={7: 0, 8: 1} if kept else {},
        compiler_params=pltpu.CompilerParams(vmem_limit_bytes=VMEM_BYTES),
        cost_estimate=pl.CostEstimate(
            flops=0, bytes_accessed=4 * 10 * rows * width, transcendentals=0
        ),
        name="grads_chunk",
    )(position, *(x for x, _ in pieces), gate, up, *kept)


def hidden_kernel(position, gate, up, *outs):
    gate_float = gate[...].astype(jnp.float32)
    activated = gate_float * jax.nn.sigmoid(gate_float)
    hidden = (activated * up[...].astype(jnp.float32)).astype(jnp.bfloat16)
    for d, out in enumerate(outs):

        @pl.when(pl.program_id(0) == d)
        def _():
            out[...] = hidden


def hidden_quarters(position, gate, up, quarter):
    rows = gate.shape[0]
    columns = pl.BlockSpec((rows, quarter), lambda i, position: (0, position[0] ^ i))
    return pl.pallas_call(
        hidden_kernel,
        out_shape=[jax.ShapeDtypeStruct((rows, quarter), jnp.bfloat16)] * 4,
        grid_spec=pltpu.PrefetchScalarGridSpec(
            num_scalar_prefetch=1,
            grid=(4,),
            in_specs=[columns, columns],
            out_specs=[pl.BlockSpec((rows, quarter), lambda i, position: (0, 0))] * 4,
        ),
        compiler_params=pltpu.CompilerParams(vmem_limit_bytes=VMEM_BYTES),
        cost_estimate=LIGHT,
        name="hidden_quarters",
    )(position, gate, up)


def terms_kernel(position, *refs):
    lows, hidden, (out, low) = refs[:4], refs[4:8], refs[8:]
    rows, width = lows[0].shape[1:]

    @pl.when(pl.program_id(0) == 0)
    def _():
        for e, piece in enumerate(lows):
            at = pl.multiple_of((position[0] ^ e) * width, width)
            for d in range(4):
                low[d * rows : (d + 1) * rows, pl.ds(at, width)] = piece[d ^ e]

    total = None
    for d, block in enumerate(hidden):
        term = lax.dot_general(
            low[d * rows : (d + 1) * rows, :],
            block[...],
            (((0,), (0,)), ((), ())),
            preferred_element_type=jnp.float32,
        )
        total = term if total is None else total + term
    out[...] = total


def rank_terms(position, lows, hidden):
    rows, quarter = hidden[0].shape
    rank = 4 * lows[0].shape[2]
    parts = 2 if quarter % 256 == 0 else 1
    width = quarter // parts
    return pl.pallas_call(
        terms_kernel,
        out_shape=jax.ShapeDtypeStruct((rank, quarter), jnp.float32),
        grid_spec=pltpu.PrefetchScalarGridSpec(
            num_scalar_prefetch=1,
            grid=(parts,),
            in_specs=[pl.BlockSpec(lows[0].shape, lambda i, position: (0, 0, 0))] * 4
            + [pl.BlockSpec((rows, width), lambda i, position: (0, i))] * 4,
            out_specs=pl.BlockSpec((rank, width), lambda i, position: (0, i)),
            scratch_shapes=[pltpu.VMEM((4 * rows, rank), jnp.bfloat16)],
        ),
        compiler_params=pltpu.CompilerParams(vmem_limit_bytes=VMEM_BYTES),
        cost_estimate=LIGHT,
        name="rank_terms",
    )(position, *lows, *hidden)


def widen_kernel(position, *refs):
    for d, piece in enumerate(refs[:-1]):

        @pl.when(pl.program_id(0) == d)
        def _():
            refs[-1][...] = piece[0].astype(refs[-1].dtype)


def widen(position, pieces):
    _, rows, quarter = pieces[0][0].shape
    return pl.pallas_call(
        widen_kernel,
        out_shape=jax.ShapeDtypeStruct((rows, len(pieces) * quarter), jnp.float32),
        grid_spec=pltpu.PrefetchScalarGridSpec(
            num_scalar_prefetch=1,
            grid=(len(pieces),),
            in_specs=[
                pl.BlockSpec((1, rows, quarter), lambda i, position, which=which: (which, 0, 0))
                for _, which in pieces
            ],
            out_specs=pl.BlockSpec((rows, quarter), lambda i, position: (0, position[0] ^ i)),
        ),
        compiler_params=pltpu.CompilerParams(vmem_limit_bytes=VMEM_BYTES),
        cost_estimate=LIGHT,
        name="projected_grad",
    )(position, *(x for x, _ in pieces))


def line(cotangent, gate_pre, up_pre, down_weight, projector):
    replicas, shards, tensors = (lax.axis_size(a) for a in AXES)
    r, f, t = (lax.axis_index(a) for a in AXES)
    rows = cotangent.shape[0]
    quarter = down_weight.shape[0] // replicas
    block = down_weight.shape[1]
    bf16, f32 = jnp.bfloat16, jnp.float32

    def send(x, move, sends=lambda a, b, c: True):
        pairs = []
        for a in range(replicas):
            for b in range(shards):
                for c in range(tensors):
                    here = (a * shards + b) * tensors + c
                    there = ((a ^ move[0]) * shards + (b ^ move[1])) * tensors + (c ^ move[2])
                    if sends(a, b, c):
                        pairs.append((here, there))
        return lax.ppermute(x, AXES, pairs)

    def after(x, *earlier):
        return lax.optimization_barrier((x, *earlier))[0]

    along, beyond, over_tensor = (0, 1, 0), (0, 2, 0), (0, 0, 1)
    odd, high = f % 2, f // 2
    position = jnp.stack([r, high]).astype(jnp.int32)
    unit = 256 if quarter % 256 == 0 else 128
    plan = chunk_plan(quarter, unit, 4)

    def total_of(first, kept, parts):
        return join([plan[first + i][1] for i in range(len(kept))], kept, parts)

    def over_replicas(total, *earlier):
        return send(after(total[2], *earlier), (2, 0, 0))

    def over_cores(total, arrived, *earlier):
        x = jnp.concatenate([total[1], arrived[1:]], axis=0)
        return send(after(x, *earlier), (1, 0, 0))

    def finish(k, total, arrived, last, written):
        pieces = [(total[0], 0), (last, 0), (arrived, 0), (last, 1)]
        return grads(position, pieces, gate_pre, up_pre, written, plan[k][0], quarter, unit)

    own_rows = [
        lax.dynamic_slice_in_dim(down_weight, r * quarter + offset, count, 0)
        for offset, count in plan
    ]

    def chunk(k, tokens, kind, columns=(), cost=0):
        return mix(
            position, tokens, down_weight, quarter, plan[k], unit, cross[k], columns, kind, cost
        )

    mine = lax.dynamic_slice_in_dim(cotangent, odd * block, block, 1)
    give = lax.dynamic_slice_in_dim(cotangent, (1 - odd) * block, block, 1)
    given = send(give, along)
    halves = [projector[:block], projector[block:]]
    found = jnp.where(odd == 0, halves[0], halves[1])
    for d in (1, 2, 3):
        x = jnp.where((odd == 0) == (d == 2), halves[0], halves[1])
        column = send(x, (0, d, 0), lambda a, b, c: a == b)
        found = jnp.where(r ^ f == d, column, found)
    def everyone(x):
        return lax.all_gather(x, ("replica", "tensor")).reshape((replicas, tensors) + x.shape)

    theirs_all = everyone(after(given, found))
    mine_all = everyone(after(mine, given, found))
    hidden = hidden_quarters(position, gate_pre, up_pre, quarter)
    tick = (given, found)
    light, heavy = 0, 16 * rows * block * plan[0][1]

    cross = [send(after(own_rows[0], *tick), beyond)]
    theirs = send(after(found, *tick), over_tensor)
    columns = [jnp.where(t == 0, found, theirs), jnp.where(t == 0, theirs, found)]
    met = {1: send(after(hidden[1], *tick), (1, 0, 0))}
    sent = [chunk(0, after(theirs_all, met[1]), bf16, columns, heavy)]
    tick = (sent[0], met[1])

    cross.append(send(after(own_rows[1], cross[0], theirs_all, *columns, met[1]), beyond))
    parts = [send(after(sent[0], *tick), along)]
    met[2] = send(after(hidden[2], *tick), (2, 0, 0))
    met[3] = send(after(hidden[3], *tick), (3, 0, 0))
    kept = [chunk(0, after(mine_all, *tick), f32, columns, light)]
    sent.append(chunk(1, after(theirs_all, *tick), bf16, (), 2 * heavy))
    tick = (sent[1], parts[0], met[2], met[3], kept[0])

    cross.append(send(after(own_rows[2], cross[1], *tick[1:]), beyond))
    parts.append(send(after(sent[1], *tick), along))
    width = plan[0][1]
    low = (kept[0][:, :, width:] + after(parts[0], *tick)[:, :, width:].astype(f32)).astype(bf16)
    lows = [low] + [send(low, (d, 0, 0)) for d in (1, 2, 3)]
    kept.append(chunk(1, after(mine_all, *tick), f32, (), light))
    total = rank_terms(position, after(lows, kept[1]), [hidden[0], met[1], met[2], met[3]])
    piece = 4 * low.shape[2] // shards
    total = total.reshape(2, 2, piece, quarter)
    theirs = jnp.where(odd == 0, total[:, 1], total[:, 0]).astype(bf16)
    total = jnp.where(odd == 0, total[:, 0], total[:, 1])
    sent.append(chunk(2, after(theirs_all, *tick), bf16, (), 3 * heavy))
    tick = (sent[2], theirs, parts[1])

    cross.append(send(after(own_rows[3], cross[2], *tick[1:]), beyond))
    stage = send(after(theirs, *tick), along)
    parts.append(send(after(sent[2], *tick), along))
    first = total_of(0, after(kept, *tick), parts[:2])
    first_y = over_replicas(first)
    kept.append(chunk(2, after(mine_all, *tick), f32, (), light))
    sent.append(chunk(3, after(theirs_all, *tick), bf16, (), 8 * heavy))
    total = total + after(stage, sent[3]).astype(f32)
    theirs = jnp.where(high == 0, total[1], total[0]).astype(bf16)
    total = jnp.where(high == 0, total[0], total[1])
    tick = (theirs, kept[2], parts[2], first_y)

    crossed = send(after(theirs, *tick), beyond)
    parts.append(send(after(sent[3], *tick), along))
    first_home = over_cores(first, first_y, *tick)
    second = total_of(2, after(kept[2:], *tick), parts[2:3])
    second_y = over_replicas(second)
    kept.append(chunk(3, after(mine_all, *tick), f32, (), light))
    scale_factor = 1.0 / math.sqrt(rows * replicas * shards)
    final = ((total + crossed.astype(f32)) * scale_factor).astype(bf16)
    tick = (final, parts[3], kept[3], first_home, second_y)

    over_y = send(after(final, *tick), (2, 0, 0))
    second_home = over_cores(second, second_y, *tick)
    third = total_of(3, after(kept[3:], *tick), parts[3:])
    third_y = over_replicas(third)
    written = finish(0, first, first_y, first_home, ())
    written = finish(2, second, second_y, second_home, written)
    tick = (over_y, third_y, written[0])

    two = jnp.stack([final, over_y])
    other = send(after(two, *tick), (1, 0, 0))
    third_home = over_cores(third, third_y, *tick)
    kept = finish(3, third, third_y, third_home, written)
    projected_grad = widen(position, ((two, 0), (other, 0), (two, 1), (other, 1)))
    return (kept[0], kept[1], projected_grad)


def solution(mesh):
    sizes = tuple(mesh.shape[a] for a in AXES)
    placed = (
        P(("replica", "fsdp"), "tensor"),
        P(("replica", "fsdp"), "tensor"),
        P(("replica", "fsdp"), "tensor"),
        P("tensor", "fsdp"),
        P("tensor", "fsdp"),
    )
    return jax.shard_map(
        line if sizes == (4, 4, 2) else general,
        mesh=mesh,
        in_specs=placed,
        out_specs=(
            P(("replica", "fsdp"), "tensor"),
            P(("replica", "fsdp"), "tensor"),
            P("fsdp", "tensor"),
        ),
        check_vma=False,
    )
```
